32 devices in a mesh: dp: 4 (over x, core), seq: 8 (over z, y).
Axes of the slice: x: 2, y: 2, z: 4, core: 2. Of those that a mesh axis runs over, the one named last changes fastest.
Arguments:
- inputs: bfloat16 [4, 2048, 1024], P('dp', 'seq'), may hold values from -6 to 6
- cotangent: bfloat16 [4, 2048, 1024], P('dp', 'seq'), may hold values from -6 to 6
- w_qkv: bfloat16 [1024, 3072], P(('dp', 'seq')), may hold values from -0.1875 to 0.1875
- bias_q: bfloat16 [1024], P(('dp', 'seq')), may hold values from -4 to 4
- bias_v: bfloat16 [1024], P(('dp', 'seq')), may hold values from -0.4375 to 0.4375
- w_out: bfloat16 [1024, 1024], P(('dp', 'seq')), may hold values from -2 to 2
- bias_out: bfloat16 [1024], P(('dp', 'seq')), may hold values from -4 to 4
- gain_one: bfloat16 [1024], P(('dp', 'seq')), may hold values from 0.099609375 to 1.8984375
- shift_one: bfloat16 [1024], P(('dp', 'seq')), may hold values from -4 to 4
- w_in: bfloat16 [1024, 4096], P(('dp', 'seq')), may hold values from -0.1875 to 0.1875
- bias_in: bfloat16 [4096], P(('dp', 'seq')), may hold values from -4 to 4
- w_back: bfloat16 [4096, 1024], P(('dp', 'seq')), may hold values from -0.09375 to 0.09375
- bias_back: bfloat16 [1024], P(('dp', 'seq')), may hold values from -4 to 4
- gain_two: bfloat16 [1024], P(('dp', 'seq')), may hold values from 0.099609375 to 1.8984375
- shift_two: bfloat16 [1024], P(('dp', 'seq')), may hold values from -4 to 4
Outputs:
- mixed: bfloat16 [4, 2048, 1024], P('dp', 'seq')
- input_grad: float32 [4, 2048, 1024], P('dp', 'seq')
- grad_w_qkv: float32 [1024, 3072], P(('dp', 'seq'))
- grad_bias_q: float32 [1024], P(('dp', 'seq'))
- grad_bias_v: float32 [1024], P(('dp', 'seq'))
- grad_w_out: float32 [1024, 1024], P(('dp', 'seq'))
- grad_bias_out: float32 [1024], P(('dp', 'seq'))
- grad_gain_one: float32 [1024], P(('dp', 'seq'))
- grad_shift_one: float32 [1024], P(('dp', 'seq'))
- grad_w_in: float32 [1024, 4096], P(('dp', 'seq'))
- grad_bias_in: float32 [4096], P(('dp', 'seq'))
- grad_w_back: float32 [4096, 1024], P(('dp', 'seq'))
- grad_bias_back: float32 [1024], P(('dp', 'seq'))
- grad_gain_two: float32 [1024], P(('dp', 'seq'))
- grad_shift_two: float32 [1024], P(('dp', 'seq'))
The draws below stay inside these ranges and needn't reach their ends.
All inputs are finite; a program needn't handle non-finite values.
Results may differ from the reference program's by a relative error of at most 0.024.
Values may be sent and summed in bfloat16 or wider, within the bound.
A program may use at most 192 MiB of HBM per device.

```python
import jax
import jax.numpy as jnp
from jax import lax

D = 1024
H = 16
HD = 64
FF = 4096
SEQS = 4
LENGTH = 2048


def shard_levels(rng, dims, split, low, high):
    def one(position, shards_of):
        heights = jax.random.uniform(jax.random.fold_in(jax.random.fold_in(rng, 6), position), (shards_of,), jnp.float32, low / len(split), high / len(split))
        return jnp.repeat(jnp.exp(heights), dims[position] // shards_of).reshape((-1,) + (1,) * (len(dims) - position - 1))

    gain = one(*split[0])
    for cut in split[1:]:
        gain = gain * one(*cut)
    return gain


def normal_values(own_key, shape, spread, reach, split=(), kind=jnp.bfloat16):
    values = spread * jax.random.normal(own_key, shape, jnp.float32)
    if split:
        values = values * shard_levels(own_key, shape, split, -0.22, 0.18)
    return jnp.clip(values, -reach, reach).astype(kind)


def setup_inputs(seed: int = 0) -> dict:
    streams_of = jax.random.split(jax.random.key(seed), 16)
    inputs = normal_values(streams_of[0], (SEQS, LENGTH, D), 1.0, 6.0, ((0, 4), (1, 8)))
    cotangent = normal_values(streams_of[1], (SEQS, LENGTH, D), 1.0, 6.0, ((0, 4), (1, 8)))
    w_qkv = normal_values(streams_of[2], (D, 3 * D), D ** -0.5, 0.1875, ((0, 32),))
    bias_q = normal_values(streams_of[3], (D,), 0.3, 4.0, ((0, 32),))
    bias_v = normal_values(streams_of[4], (D,), 0.03, 0.4375, ((0, 32),))
    w_out = normal_values(streams_of[5], (D, D), (max(1, D * 16 // LENGTH)) ** -0.5, 2.0, ((0, 32),))
    bias_out = normal_values(streams_of[6], (D,), 0.3, 4.0, ((0, 32),))
    gain_one = jnp.clip(1.0 + 0.18 * jax.random.normal(streams_of[7], (D,), jnp.float32), 0.099609375, 1.8984375).astype(jnp.bfloat16)
    shift_one = normal_values(streams_of[8], (D,), 0.3, 4.0, ((0, 32),))
    w_in = normal_values(streams_of[9], (D, FF), D ** -0.5, 0.1875, ((0, 32),))
    bias_in = normal_values(streams_of[10], (FF,), 0.3, 4.0, ((0, 32),))
    w_back = normal_values(streams_of[11], (FF, D), FF ** -0.5, 0.09375, ((0, 32),))
    bias_back = normal_values(streams_of[12], (D,), 0.3, 4.0, ((0, 32),))
    gain_two = jnp.clip(1.0 + 0.18 * jax.random.normal(streams_of[13], (D,), jnp.float32), 0.099609375, 1.8984375).astype(jnp.bfloat16)
    shift_two = normal_values(streams_of[14], (D,), 0.3, 4.0, ((0, 32),))
    return {"inputs": inputs, "cotangent": cotangent, "w_qkv": w_qkv, "bias_q": bias_q, "bias_v": bias_v, "w_out": w_out, "bias_out": bias_out, "gain_one": gain_one, "shift_one": shift_one, "w_in": w_in, "bias_in": bias_in, "w_back": w_back, "bias_back": bias_back, "gain_two": gain_two, "shift_two": shift_two}


EPSILON = 1e-06
HIGH = lax.Precision.HIGHEST

@jax.custom_vjp
def low(v):
    return lax.optimization_barrier(v.astype(jnp.bfloat16)).astype(jnp.float32)

@jax.custom_vjp
def low_back(v):
    return v

def low_keep(v):
    return (low(v), None)

def low_pass(kept, grad):
    return (grad,)

def back_keep(v):
    return (v, None)

def back_low(kept, grad):
    return (low(grad),)
low.defvjp(low_keep, low_pass)
low_back.defvjp(back_keep, back_low)

def product(left, right):
    return jnp.dot(left, right, precision=HIGH)

def layer_norm(values, gain_row, shift_row):
    row_mean = lax.optimization_barrier(jnp.mean(values, axis=-1, keepdims=True))
    centered = values - row_mean
    variance = lax.optimization_barrier(jnp.mean(centered * centered, axis=-1, keepdims=True))
    return centered * lax.rsqrt(variance + EPSILON) * gain_row + shift_row

def gelu_exact(values):
    return 0.5 * values * (1.0 + lax.erf(values * 0.7071067811865476))

def one_sequence(sequence, params):
    w_qkv, bias_q, bias_v, w_out, bias_out, gain_one, shift_one, w_in, bias_in, w_back, bias_back, gain_two, shift_two = params
    projected = product(low(sequence), w_qkv)
    queries = low_back(low(projected[:, :D] + bias_q)).reshape(LENGTH, H, HD)
    key_rows = low_back(low(projected[:, D:2 * D])).reshape(LENGTH, H, HD)
    value_rows = low_back(low(projected[:, 2 * D:] + bias_v)).reshape(LENGTH, H, HD)
    block_rows = min(512, LENGTH)

    def attend_block(query_block):
        scores = low_back(jnp.einsum('qhd,khd->hqk', query_block, key_rows, precision=HIGH) * HD ** (-0.5))
        shifted = jnp.exp(scores - lax.optimization_barrier(jnp.max(scores, axis=-1, keepdims=True)))
        soft_weights = shifted / lax.optimization_barrier(jnp.sum(shifted, axis=-1, keepdims=True))
        return jnp.einsum('hqk,khd->qhd', low(soft_weights), value_rows, precision=HIGH)
    blocks = lax.map(jax.checkpoint(attend_block), queries.reshape(LENGTH // block_rows, block_rows, H, HD))
    attended = low_back(low(blocks.reshape(LENGTH, D)))
    hidden = sequence + low_back(product(attended, w_out)) + bias_out
    first = layer_norm(hidden, gain_one, shift_one)
    inner = low_back(product(low(first), w_in) + bias_in)
    gated = low(gelu_exact(inner))
    result = first + low_back(product(gated, w_back)) + bias_back
    return layer_norm(result, gain_two, shift_two)

def reference(inputs, cotangent, w_qkv, bias_q, bias_v, w_out, bias_out, gain_one, shift_one, w_in, bias_in, w_back, bias_back, gain_two, shift_two):
    params = tuple((item.astype(jnp.float32) for item in (w_qkv, bias_q, bias_v, w_out, bias_out, gain_one, shift_one, w_in, bias_in, w_back, bias_back, gain_two, shift_two)))

    def forward(sequences, weights):
        return lax.map(lambda sequence: one_sequence(sequence, weights), sequences)
    mixed, pullback = jax.vjp(forward, inputs.astype(jnp.float32), params)
    input_grad, weight_grads = pullback(cotangent.astype(jnp.float32))
    grad_w_qkv, grad_bias_q, grad_bias_v, grad_w_out, grad_bias_out, grad_gain_one, grad_shift_one, grad_w_in, grad_bias_in, grad_w_back, grad_bias_back, grad_gain_two, grad_shift_two = weight_grads
    return (mixed.astype(jnp.bfloat16), input_grad, grad_w_qkv, grad_bias_q, grad_bias_v, grad_w_out, grad_bias_out, grad_gain_one, grad_shift_one, grad_w_in, grad_bias_in, grad_w_back, grad_bias_back, grad_gain_two, grad_shift_two)
```

```python
import jax
import jax.numpy as jnp
from jax import lax
from jax.experimental import pallas as pl
from jax.experimental.pallas import tpu as pltpu
from jax.sharding import PartitionSpec as P

D = 1024
H = 16
HD = 64


EPSILON = 1e-06
ROOT_HALF = 0.7071067811865476
INV_ROOT_TAU = 0.3989422804014327
SCALE = HD ** (-0.5)
SCALE_LOG2 = SCALE * 1.4426950408889634
VMEM_LIMIT = 48 * 1024 * 1024
AXES = ("dp", "seq")


def layer_stats(values):
    row_mean = jnp.mean(values, axis=-1, keepdims=True)
    centered = values - row_mean
    inv_std = lax.rsqrt(jnp.mean(centered * centered, axis=-1, keepdims=True) + EPSILON)
    return (centered * inv_std, inv_std)


def norm_back(grad_rows, normed, inv_std, gain_row):
    scaled = grad_rows * gain_row
    return inv_std * (
        scaled
        - jnp.mean(scaled, axis=-1, keepdims=True)
        - normed * jnp.mean(scaled * normed, axis=-1, keepdims=True)
    )


def gelu_exact(values):
    return 0.5 * values * (1.0 + lax.erf(values * ROOT_HALF))


def gelu_slope(values):
    return (
        0.5 * (1.0 + lax.erf(values * ROOT_HALF))
        + values * jnp.exp(-0.5 * values * values) * INV_ROOT_TAU
    )


def dense(left, right):
    return jnp.dot(left, right, preferred_element_type=jnp.float32)


def dense_left_t(left, right):
    return lax.dot_general(
        left, right, (((0,), (0,)), ((), ())), preferred_element_type=jnp.float32
    )


def dense_right_t(left, right):
    return lax.dot_general(
        left, right, (((1,), (1,)), ((), ())), preferred_element_type=jnp.float32
    )


def mm(left, right, dims):
    return lax.dot_general(left, right, (dims, ((), ())), preferred_element_type=jnp.float32)


def head_only(block, head):
    lane = lax.broadcasted_iota(jnp.int32, block.shape, 1)
    inside = (lane >= head * HD) & (lane < (head + 1) * HD)
    return jnp.where(inside, block, jnp.zeros_like(block))


def attend_forward_body(q_ref, k_ref, v_ref, low_ref, full_ref, lse_ref, vt_ref):
    groups, _, rows, width = k_ref.shape
    length = groups * rows

    @pl.when(pl.program_id(0) == 0)
    def _():
        vt_ref[...] = v_ref[...].reshape(length, width).T

    keys = k_ref[...].reshape(length, width)
    queries = q_ref[0, 0]
    outs = []
    for head in range(width // HD):
        scores = mm(keys, head_only(queries, head), ((1,), (1,)))
        top = jnp.max(scores, axis=0, keepdims=True) * SCALE_LOG2
        weights = jnp.exp2(scores * SCALE_LOG2 - top)
        total = jnp.sum(weights, axis=0, keepdims=True)
        out_t = mm(vt_ref[head * HD : (head + 1) * HD, :], weights.astype(jnp.bfloat16), ((1,), (0,)))
        outs.append(out_t / total)
        lse_ref[0, head : head + 1, :] = top + jnp.log2(total)
    out = jnp.concatenate(outs, axis=0).T
    full_ref[0] = out
    low_ref[0] = out.astype(jnp.bfloat16)


def attend_forward(packed):
    groups, _, rows, width = packed.shape
    heads = width // HD
    whole = lambda which: pl.BlockSpec((groups, 1, rows, width), lambda i: (0, which, 0, 0))
    own = pl.BlockSpec((1, rows, width), lambda i: (i, 0, 0))
    length = groups * rows
    return pl.pallas_call(
        attend_forward_body,
        grid=(groups,),
        in_specs=[pl.BlockSpec((1, 1, rows, width), lambda i: (i, 0, 0, 0)), whole(1), whole(2)],
        out_specs=[own, own, pl.BlockSpec((1, heads, rows), lambda i: (i, 0, 0))],
        out_shape=[
            jax.ShapeDtypeStruct((groups, rows, width), jnp.bfloat16),
            jax.ShapeDtypeStruct((groups, rows, width), jnp.float32),
            jax.ShapeDtypeStruct((groups, heads, rows), jnp.float32),
        ],
        scratch_shapes=[pltpu.VMEM((width, length), jnp.bfloat16)],
        compiler_params=pltpu.CompilerParams(vmem_limit_bytes=VMEM_LIMIT),
        cost_estimate=pl.CostEstimate(
            flops=16 * length * length * width,
            bytes_accessed=10 * length * width,
            transcendentals=heads * length * length,
        ),
        name="attend_forward",
    )(packed, packed, packed)


def attend_backward_body(
    q_ref, k_ref, v_ref, grad_ref, full_ref, lse_ref, out_ref, kt_ref, dk_ref, dv_ref
):
    groups, _, rows, width = k_ref.shape
    length = groups * rows
    heads = width // HD
    step = pl.program_id(0)

    @pl.when(step == 0)
    def _():
        kt_ref[...] = k_ref[...].reshape(length, width).T
        dk_ref[...] = jnp.zeros_like(dk_ref)
        dv_ref[...] = jnp.zeros_like(dv_ref)

    queries = q_ref[0, 0]
    grads = grad_ref[0]
    spread = (grads.astype(jnp.float32) * full_ref[0]).T
    q_heads = [head_only(queries, head) for head in range(heads)]
    g_heads = [head_only(grads, head) for head in range(heads)]
    deltas = [
        jnp.sum(spread[head * HD : (head + 1) * HD], axis=0, keepdims=True)
        for head in range(heads)
    ]
    dq = [jnp.zeros((HD, rows), jnp.float32) for _ in range(heads)]
    per = min(2, groups)
    piece = per * rows
    for part in range(groups // per):
        keys = k_ref[part * per : (part + 1) * per].reshape(piece, width)
        values = v_ref[part * per : (part + 1) * per].reshape(piece, width)
        span = slice(part * piece, (part + 1) * piece)
        dk_part = dk_ref[span, :]
        dv_part = dv_ref[span, :]
        for head in range(heads):
            scores = mm(keys, q_heads[head], ((1,), (1,)))
            weights = jnp.exp2(scores * SCALE_LOG2 - lse_ref[0, head : head + 1, :])
            d_soft = mm(values, g_heads[head], ((1,), (1,)))
            d_scores = (weights * (d_soft - deltas[head])).astype(jnp.bfloat16)
            dv_part += mm(weights.astype(jnp.bfloat16), g_heads[head], ((1,), (0,)))
            dk_part += mm(d_scores, q_heads[head], ((1,), (0,)))
            dq[head] += mm(kt_ref[head * HD : (head + 1) * HD, span], d_scores, ((1,), (0,)))
        dk_ref[span, :] = dk_part
        dv_ref[span, :] = dv_part
    dq_all = jnp.concatenate(dq, axis=0) if heads > 1 else dq[0]
    out_ref[step, 0] = (dq_all * SCALE).T.astype(jnp.bfloat16)

    @pl.when(step == groups - 1)
    def _():
        out_ref[:, 1] = (dk_ref[...] * SCALE).astype(jnp.bfloat16).reshape(groups, rows, width)
        out_ref[:, 2] = dv_ref[...].astype(jnp.bfloat16).reshape(groups, rows, width)


def attend_backward(packed, grads, full, lse):
    groups, _, rows, width = packed.shape
    heads = width // HD
    length = groups * rows
    whole = lambda which: pl.BlockSpec((groups, 1, rows, width), lambda i: (0, which, 0, 0))
    own = pl.BlockSpec((1, rows, width), lambda i: (i, 0, 0))
    return pl.pallas_call(
        attend_backward_body,
        grid=(groups,),
        in_specs=[
            pl.BlockSpec((1, 1, rows, width), lambda i: (i, 0, 0, 0)),
            whole(1),
            whole(2),
            own,
            own,
            pl.BlockSpec((1, heads, rows), lambda i: (i, 0, 0)),
        ],
        out_specs=pl.BlockSpec((groups, 3, rows, width), lambda i: (0, 0, 0, 0)),
        out_shape=jax.ShapeDtypeStruct((groups, 3, rows, width), jnp.bfloat16),
        scratch_shapes=[
            pltpu.VMEM((width, length), jnp.bfloat16),
            pltpu.VMEM((length, width), jnp.float32),
            pltpu.VMEM((length, width), jnp.float32),
        ],
        compiler_params=pltpu.CompilerParams(vmem_limit_bytes=VMEM_LIMIT),
        cost_estimate=pl.CostEstimate(
            flops=40 * length * length * width,
            bytes_accessed=20 * length * width,
            transcendentals=heads * length * length,
        ),
        name="attend_backward",
    )(packed, packed, packed, grads, full, lse)


def swap(blocks):
    return lax.all_to_all(blocks, "seq", 0, 0, tiled=True)


def gather(shard):
    return lax.all_gather(shard, AXES, axis=0, tiled=True)


def scatter(whole):
    return lax.psum_scatter(whole, AXES, scatter_dimension=0, tiled=True)


def per_device(
    inputs,
    cotangent,
    w_qkv,
    bias_q,
    bias_v,
    w_out,
    bias_out,
    gain_one,
    shift_one,
    w_in,
    bias_in,
    w_back,
    bias_back,
    gain_two,
    shift_two,
):
    groups = lax.axis_size("seq")
    devices = lax.axis_size("dp") * groups
    vectors = (bias_q, bias_v, bias_out, gain_one, shift_one, bias_in, bias_back, gain_two, shift_two)
    wide_qkv = gather(w_qkv)
    rows_of = lax.all_gather(jnp.concatenate(vectors), AXES, axis=0, tiled=False)
    wide_out = gather(w_out)
    wide_in = gather(w_in)
    wide_back = gather(w_back)
    full = []
    place = 0
    for vector in vectors:
        part = rows_of[:, place : place + vector.shape[0]]
        full.append(part.reshape(1, -1).astype(jnp.float32))
        place += vector.shape[0]
    full_bq, full_bv, full_bo, full_g1, full_s1, full_b1, full_b2, full_g2, full_s2 = full

    sequence = inputs[0]
    rows_here = sequence.shape[0]
    width = D // groups
    bias_qkv = jnp.concatenate([full_bq, jnp.zeros_like(full_bq), full_bv], axis=1)
    projected = (dense(sequence, wide_qkv) + bias_qkv).astype(jnp.bfloat16)
    packed = swap(jnp.transpose(projected.reshape(rows_here, 3, groups, width), (2, 1, 0, 3)))
    att_low, att_full, lse = attend_forward(packed)
    attended = jnp.transpose(swap(att_low), (1, 0, 2)).reshape(rows_here, D)

    hidden = sequence.astype(jnp.float32) + dense(attended, wide_out) + full_bo
    normed_one, inv_one = layer_stats(hidden)
    first = normed_one * full_g1 + full_s1
    first_low = first.astype(jnp.bfloat16)
    inner = dense(first_low, wide_in) + full_b1
    gated = gelu_exact(inner).astype(jnp.bfloat16)
    result = first + dense(gated, wide_back) + full_b2
    normed_two, inv_two = layer_stats(result)
    mixed = (normed_two * full_g2 + full_s2).astype(jnp.bfloat16)

    grad_rows = cotangent[0].astype(jnp.float32)
    grad_gain_two = jnp.sum(grad_rows * normed_two, axis=0)
    grad_shift_two = jnp.sum(grad_rows, axis=0)
    grad_result = norm_back(grad_rows, normed_two, inv_two, full_g2)
    grad_bias_back = jnp.sum(grad_result, axis=0)
    result_low = grad_result.astype(jnp.bfloat16)
    own_back = scatter(dense_left_t(gated, result_low).astype(jnp.bfloat16))
    grad_inner = (dense_right_t(result_low, wide_back) * gelu_slope(inner)).astype(jnp.bfloat16)
    grad_bias_in = jnp.sum(grad_inner.astype(jnp.float32), axis=0)
    own_in = scatter(dense_left_t(first_low, grad_inner).astype(jnp.bfloat16))
    grad_first = grad_result + dense_right_t(grad_inner, wide_in)
    grad_gain_one = jnp.sum(grad_first * normed_one, axis=0)
    grad_shift_one = jnp.sum(grad_first, axis=0)
    grad_hidden = norm_back(grad_first, normed_one, inv_one, full_g1)
    grad_bias_out = jnp.sum(grad_hidden, axis=0)
    hidden_low = grad_hidden.astype(jnp.bfloat16)
    own_out = scatter(dense_left_t(attended, hidden_low).astype(jnp.bfloat16))
    grad_att = dense_right_t(hidden_low, wide_out).astype(jnp.bfloat16)
    grad_heads = swap(jnp.transpose(grad_att.reshape(rows_here, groups, width), (1, 0, 2)))
    grad_packed = swap(attend_backward(packed, grad_heads, att_full, lse))
    grad_proj = jnp.transpose(grad_packed, (2, 1, 0, 3)).reshape(rows_here, 3 * D)
    own_qkv = scatter(dense_left_t(sequence, grad_proj).astype(jnp.bfloat16))
    grad_bias_q = jnp.sum(grad_proj[:, :D].astype(jnp.float32), axis=0)
    grad_bias_v = jnp.sum(grad_proj[:, 2 * D :].astype(jnp.float32), axis=0)
    input_grad = grad_hidden + dense_right_t(grad_proj, wide_qkv)

    sums = (
        grad_bias_q,
        grad_bias_v,
        grad_bias_out,
        grad_gain_one,
        grad_shift_one,
        grad_bias_in,
        grad_bias_back,
        grad_gain_two,
        grad_shift_two,
    )
    owned = lax.psum_scatter(
        jnp.concatenate([item.reshape(devices, -1) for item in sums], axis=1),
        AXES,
        scatter_dimension=0,
        tiled=False,
    )
    small = []
    place = 0
    for vector in vectors:
        small.append(owned[place : place + vector.shape[0]])
        place += vector.shape[0]
    own_bq, own_bv, own_bo, own_g1, own_s1, own_b1, own_b2, own_g2, own_s2 = small
    return (
        mixed[None],
        input_grad[None],
        own_qkv.astype(jnp.float32),
        own_bq,
        own_bv,
        own_out.astype(jnp.float32),
        own_bo,
        own_g1,
        own_s1,
        own_in.astype(jnp.float32),
        own_b1,
        own_back.astype(jnp.float32),
        own_b2,
        own_g2,
        own_s2,
    )


def solution(mesh):
    return jax.shard_map(
        per_device,
        mesh=mesh,
        in_specs=(
            P("dp", "seq", None),
            P("dp", "seq", None),
            P(("dp", "seq"), None),
            P(("dp", "seq")),
            P(("dp", "seq")),
            P(("dp", "seq"), None),
            P(("dp", "seq")),
            P(("dp", "seq")),
            P(("dp", "seq")),
            P(("dp", "seq"), None),
            P(("dp", "seq")),
            P(("dp", "seq"), None),
            P(("dp", "seq")),
            P(("dp", "seq")),
            P(("dp", "seq")),
        ),
        out_specs=(
            P("dp", "seq", None),
            P("dp", "seq", None),
            P(("dp", "seq"), None),
            P(("dp", "seq")),
            P(("dp", "seq")),
            P(("dp", "seq"), None),
            P(("dp", "seq")),
            P(("dp", "seq")),
            P(("dp", "seq")),
            P(("dp", "seq"), None),
            P(("dp", "seq")),
            P(("dp", "seq"), None),
            P(("dp", "seq")),
            P(("dp", "seq")),
            P(("dp", "seq")),
        ),
        check_vma=False,
    )
```

```python
import jax
import jax.numpy as jnp
from jax import lax
from jax.experimental import pallas as pl
from jax.experimental.pallas import tpu as pltpu
from jax.sharding import PartitionSpec as P

D = 1024
H = 16
HD = 64


EPSILON = 1e-06
ROOT_HALF = 0.7071067811865476
INV_ROOT_TAU = 0.3989422804014327
SCALE = HD ** (-0.5)
SCALE_LOG2 = SCALE * 1.4426950408889634
VMEM_LIMIT = 48 * 1024 * 1024
AXES = ("dp", "seq")


def layer_stats(values):
    row_mean = jnp.mean(values, axis=-1, keepdims=True)
    centered = values - row_mean
    inv_std = lax.rsqrt(jnp.mean(centered * centered, axis=-1, keepdims=True) + EPSILON)
    return (centered * inv_std, inv_std)


def norm_back(grad_rows, normed, inv_std, gain_row):
    scaled = grad_rows * gain_row
    return inv_std * (
        scaled
        - jnp.mean(scaled, axis=-1, keepdims=True)
        - normed * jnp.mean(scaled * normed, axis=-1, keepdims=True)
    )


def gelu_exact(values):
    return 0.5 * values * (1.0 + lax.erf(values * ROOT_HALF))


def gelu_slope(values):
    return (
        0.5 * (1.0 + lax.erf(values * ROOT_HALF))
        + values * jnp.exp(-0.5 * values * values) * INV_ROOT_TAU
    )


def dense(left, right):
    return jnp.dot(left, right, preferred_element_type=jnp.float32)


def dense_left_t(left, right):
    return lax.dot_general(
        left, right, (((0,), (0,)), ((), ())), preferred_element_type=jnp.float32
    )


def dense_right_t(left, right):
    return lax.dot_general(
        left, right, (((1,), (1,)), ((), ())), preferred_element_type=jnp.float32
    )


def mm(left, right, dims):
    return lax.dot_general(left, right, (dims, ((), ())), preferred_element_type=jnp.float32)


def head_only(block, head):
    lane = lax.broadcasted_iota(jnp.int32, block.shape, 1)
    inside = (lane >= head * HD) & (lane < (head + 1) * HD)
    return jnp.where(inside, block, jnp.zeros_like(block))


def attend_forward_body(q_ref, k_ref, v_ref, low_ref, full_ref, lse_ref, vt_ref):
    groups, _, rows, width = k_ref.shape
    length = groups * rows

    @pl.when(pl.program_id(0) == 0)
    def _():
        vt_ref[...] = v_ref[...].reshape(length, width).T

    keys = k_ref[...].reshape(length, width)
    queries = q_ref[0, 0]
    outs = []
    for head in range(width // HD):
        scores = mm(keys, head_only(queries, head), ((1,), (1,)))
        top = jnp.max(scores, axis=0, keepdims=True) * SCALE_LOG2
        weights = jnp.exp2(scores * SCALE_LOG2 - top)
        total = jnp.sum(weights, axis=0, keepdims=True)
        out_t = mm(vt_ref[head * HD : (head + 1) * HD, :], weights.astype(jnp.bfloat16), ((1,), (0,)))
        outs.append(out_t / total)
        lse_ref[0, head : head + 1, :] = top + jnp.log2(total)
    out = jnp.concatenate(outs, axis=0).T
    full_ref[0] = out
    low_ref[0] = out.astype(jnp.bfloat16)


def attend_forward(packed):
    groups, _, rows, width = packed.shape
    heads = width // HD
    whole = lambda which: pl.BlockSpec((groups, 1, rows, width), lambda i: (0, which, 0, 0))
    own = pl.BlockSpec((1, rows, width), lambda i: (i, 0, 0))
    length = groups * rows
    return pl.pallas_call(
        attend_forward_body,
        grid=(groups,),
        in_specs=[pl.BlockSpec((1, 1, rows, width), lambda i: (i, 0, 0, 0)), whole(1), whole(2)],
        out_specs=[own, own, pl.BlockSpec((1, heads, rows), lambda i: (i, 0, 0))],
        out_shape=[
            jax.ShapeDtypeStruct((groups, rows, width), jnp.bfloat16),
            jax.ShapeDtypeStruct((groups, rows, width), jnp.float32),
            jax.ShapeDtypeStruct((groups, heads, rows), jnp.float32),
        ],
        scratch_shapes=[pltpu.VMEM((width, length), jnp.bfloat16)],
        compiler_params=pltpu.CompilerParams(vmem_limit_bytes=VMEM_LIMIT),
        cost_estimate=pl.CostEstimate(
            flops=16 * length * length * width,
            bytes_accessed=10 * length * width,
            transcendentals=heads * length * length,
        ),
        name="attend_forward",
    )(packed, packed, packed)


def attend_backward_body(
    q_ref, k_ref, v_ref, grad_ref, full_ref, lse_ref, out_ref, kt_ref, dk_ref, dv_ref
):
    groups, _, rows, width = k_ref.shape
    length = groups * rows
    heads = width // HD
    step = pl.program_id(0)

    @pl.when(step == 0)
    def _():
        kt_ref[...] = k_ref[...].reshape(length, width).T
        dk_ref[...] = jnp.zeros_like(dk_ref)
        dv_ref[...] = jnp.zeros_like(dv_ref)

    queries = q_ref[0, 0]
    grads = grad_ref[0]
    spread = (grads.astype(jnp.float32) * full_ref[0]).T
    q_heads = [head_only(queries, head) for head in range(heads)]
    g_heads = [head_only(grads, head) for head in range(heads)]
    deltas = [
        jnp.sum(spread[head * HD : (head + 1) * HD], axis=0, keepdims=True)
        for head in range(heads)
    ]
    dq = [jnp.zeros((HD, rows), jnp.float32) for _ in range(heads)]
    per = min(2, groups)
    piece = per * rows
    for part in range(groups // per):
        keys = k_ref[part * per : (part + 1) * per].reshape(piece, width)
        values = v_ref[part * per : (part + 1) * per].reshape(piece, width)
        span = slice(part * piece, (part + 1) * piece)
        dk_part = dk_ref[span, :]
        dv_part = dv_ref[span, :]
        for head in range(heads):
            scores = mm(keys, q_heads[head], ((1,), (1,)))
            weights = jnp.exp2(scores * SCALE_LOG2 - lse_ref[0, head : head + 1, :])
            d_soft = mm(values, g_heads[head], ((1,), (1,)))
            d_scores = (weights * (d_soft - deltas[head])).astype(jnp.bfloat16)
            dv_part += mm(weights.astype(jnp.bfloat16), g_heads[head], ((1,), (0,)))
            dk_part += mm(d_scores, q_heads[head], ((1,), (0,)))
            dq[head] += mm(kt_ref[head * HD : (head + 1) * HD, span], d_scores, ((1,), (0,)))
        dk_ref[span, :] = dk_part
        dv_ref[span, :] = dv_part
    dq_all = jnp.concatenate(dq, axis=0) if heads > 1 else dq[0]
    out_ref[step, 0] = (dq_all * SCALE).T.astype(jnp.bfloat16)

    @pl.when(step == groups - 1)
    def _():
        out_ref[:, 1] = (dk_ref[...] * SCALE).astype(jnp.bfloat16).reshape(groups, rows, width)
        out_ref[:, 2] = dv_ref[...].astype(jnp.bfloat16).reshape(groups, rows, width)


def attend_backward(packed, grads, full, lse):
    groups, _, rows, width = packed.shape
    heads = width // HD
    length = groups * rows
    whole = lambda which: pl.BlockSpec((groups, 1, rows, width), lambda i: (0, which, 0, 0))
    own = pl.BlockSpec((1, rows, width), lambda i: (i, 0, 0))
    return pl.pallas_call(
        attend_backward_body,
        grid=(groups,),
        in_specs=[
            pl.BlockSpec((1, 1, rows, width), lambda i: (i, 0, 0, 0)),
            whole(1),
            whole(2),
            own,
            own,
            pl.BlockSpec((1, heads, rows), lambda i: (i, 0, 0)),
        ],
        out_specs=pl.BlockSpec((groups, 3, rows, width), lambda i: (0, 0, 0, 0)),
        out_shape=jax.ShapeDtypeStruct((groups, 3, rows, width), jnp.bfloat16),
        scratch_shapes=[
            pltpu.VMEM((width, length), jnp.bfloat16),
            pltpu.VMEM((length, width), jnp.float32),
            pltpu.VMEM((length, width), jnp.float32),
        ],
        compiler_params=pltpu.CompilerParams(vmem_limit_bytes=VMEM_LIMIT),
        cost_estimate=pl.CostEstimate(
            flops=40 * length * length * width,
            bytes_accessed=20 * length * width,
            transcendentals=heads * length * length,
        ),
        name="attend_backward",
    )(packed, packed, packed, grads, full, lse)


def swap(blocks):
    return lax.all_to_all(blocks, "seq", 0, 0, tiled=True)


def bit_order(turn):
    low = (lax.axis_size("seq") - 1).bit_length()
    bits = low + (lax.axis_size("dp") - 1).bit_length()
    near = [bits - 1, 0, 1]
    near = near[turn:] + near[:turn]
    return [low] + near + [bit for bit in range(bits) if bit != low and bit not in near]


def my_bit(bit):
    index = lax.axis_index("dp") * lax.axis_size("seq") + lax.axis_index("seq")
    return lax.rem(lax.div(index, 1 << bit), 2)


def exchange(block, bit):
    devices = lax.axis_size("dp") * lax.axis_size("seq")
    return lax.ppermute(block, AXES, [(i, i ^ (1 << bit)) for i in range(devices)])


def gather(shard, turn):
    block = shard
    held = []
    for bit in reversed(bit_order(turn)):
        other = exchange(block, bit)
        upper = my_bit(bit) == 1
        axis = sum(1 for have in held if have > bit)
        block = jnp.stack(
            [jnp.where(upper, other, block), jnp.where(upper, block, other)], axis=axis
        )
        held.append(bit)
    return block.reshape((-1,) + shard.shape[1:])


def scatter(whole, turn):
    order = bit_order(turn)
    kind = whole.dtype
    block = whole.reshape((2,) * len(order) + whole.shape[1:])
    held = sorted(order, reverse=True)
    for bit in order:
        axis = held.index(bit)
        mine = my_bit(bit)
        kept = lax.dynamic_index_in_dim(block, mine, axis, keepdims=False)
        sent = lax.dynamic_index_in_dim(block, 1 - mine, axis, keepdims=False)
        other = exchange(sent, bit)
        held.remove(bit)
        block = kept.astype(jnp.float32) + other.astype(jnp.float32)
        if held:
            block = block.astype(kind)
    return block


def scatter_rows(grad, turn):
    devices = lax.axis_size("dp") * lax.axis_size("seq")
    return scatter(grad.astype(jnp.bfloat16).reshape(devices, -1, grad.shape[1]), turn)


def per_device(
    inputs,
    cotangent,
    w_qkv,
    bias_q,
    bias_v,
    w_out,
    bias_out,
    gain_one,
    shift_one,
    w_in,
    bias_in,
    w_back,
    bias_back,
    gain_two,
    shift_two,
):
    groups = lax.axis_size("seq")
    devices = lax.axis_size("dp") * groups
    vectors = (bias_q, bias_v, bias_out, gain_one, shift_one, bias_in, bias_back, gain_two, shift_two)
    wide_qkv = [gather(w_qkv[:, part * D : (part + 1) * D], part) for part in range(3)]
    rows_of = gather(jnp.concatenate(vectors)[None], 0)
    wide_out = gather(w_out, 2)
    wide_in = gather(w_in, 1)
    wide_back = gather(w_back, 0)
    full = []
    place = 0
    for vector in vectors:
        part = rows_of[:, place : place + vector.shape[0]]
        full.append(part.reshape(1, -1).astype(jnp.float32))
        place += vector.shape[0]
    full_bq, full_bv, full_bo, full_g1, full_s1, full_b1, full_b2, full_g2, full_s2 = full

    sequence = inputs[0]
    rows_here = sequence.shape[0]
    width = D // groups
    projected = jnp.stack(
        [
            (dense(sequence, wide_qkv[0]) + full_bq).astype(jnp.bfloat16),
            dense(sequence, wide_qkv[1]).astype(jnp.bfloat16),
            (dense(sequence, wide_qkv[2]) + full_bv).astype(jnp.bfloat16),
        ]
    )
    packed = swap(jnp.transpose(projected.reshape(3, rows_here, groups, width), (2, 0, 1, 3)))
    att_low, att_full, lse = attend_forward(packed)
    attended = jnp.transpose(swap(att_low), (1, 0, 2)).reshape(rows_here, D)

    hidden = sequence.astype(jnp.float32) + dense(attended, wide_out) + full_bo
    normed_one, inv_one = layer_stats(hidden)
    first = normed_one * full_g1 + full_s1
    first_low = first.astype(jnp.bfloat16)
    inner = dense(first_low, wide_in) + full_b1
    gated = gelu_exact(inner).astype(jnp.bfloat16)
    result = first + dense(gated, wide_back) + full_b2
    normed_two, inv_two = layer_stats(result)
    mixed = (normed_two * full_g2 + full_s2).astype(jnp.bfloat16)

    grad_rows = cotangent[0].astype(jnp.float32)
    grad_gain_two = jnp.sum(grad_rows * normed_two, axis=0)
    grad_shift_two = jnp.sum(grad_rows, axis=0)
    grad_result = norm_back(grad_rows, normed_two, inv_two, full_g2)
    grad_bias_back = jnp.sum(grad_result, axis=0)
    result_low = grad_result.astype(jnp.bfloat16)
    own_back = scatter_rows(dense_left_t(gated, result_low), 0)
    grad_inner = (dense_right_t(result_low, wide_back) * gelu_slope(inner)).astype(jnp.bfloat16)
    grad_bias_in = jnp.sum(grad_inner.astype(jnp.float32), axis=0)
    own_in = scatter_rows(dense_left_t(first_low, grad_inner), 1)
    grad_first = grad_result + dense_right_t(grad_inner, wide_in)
    grad_gain_one = jnp.sum(grad_first * normed_one, axis=0)
    grad_shift_one = jnp.sum(grad_first, axis=0)
    grad_hidden = norm_back(grad_first, normed_one, inv_one, full_g1)
    grad_bias_out = jnp.sum(grad_hidden, axis=0)
    hidden_low = grad_hidden.astype(jnp.bfloat16)
    own_out = scatter_rows(dense_left_t(attended, hidden_low), 2)
    grad_att = dense_right_t(hidden_low, wide_out).astype(jnp.bfloat16)
    grad_heads = swap(jnp.transpose(grad_att.reshape(rows_here, groups, width), (1, 0, 2)))
    grad_packed = swap(attend_backward(packed, grad_heads, att_full, lse))
    grad_proj = jnp.transpose(grad_packed, (1, 2, 0, 3)).reshape(3, rows_here, D)
    own_qkv = jnp.concatenate(
        [scatter_rows(dense_left_t(sequence, grad_proj[part]), part) for part in range(3)], axis=1
    )
    grad_bias_q = jnp.sum(grad_proj[0].astype(jnp.float32), axis=0)
    grad_bias_v = jnp.sum(grad_proj[2].astype(jnp.float32), axis=0)
    input_grad = grad_hidden + sum(
        dense_right_t(grad_proj[part], wide_qkv[part]) for part in range(3)
    )

    sums = (
        grad_bias_q,
        grad_bias_v,
        grad_bias_out,
        grad_gain_one,
        grad_shift_one,
        grad_bias_in,
        grad_bias_back,
        grad_gain_two,
        grad_shift_two,
    )
    owned = scatter(
        jnp.concatenate([item.reshape(devices, -1) for item in sums], axis=1)[:, None], 0
    )[0]
    small = []
    place = 0
    for vector in vectors:
        small.append(owned[place : place + vector.shape[0]])
        place += vector.shape[0]
    own_bq, own_bv, own_bo, own_g1, own_s1, own_b1, own_b2, own_g2, own_s2 = small
    return (
        mixed[None],
        input_grad[None],
        own_qkv,
        own_bq,
        own_bv,
        own_out,
        own_bo,
        own_g1,
        own_s1,
        own_in,
        own_b1,
        own_back,
        own_b2,
        own_g2,
        own_s2,
    )


def solution(mesh):
    return jax.shard_map(
        per_device,
        mesh=mesh,
        in_specs=(
            P("dp", "seq", None),
            P("dp", "seq", None),
            P(("dp", "seq"), None),
            P(("dp", "seq")),
            P(("dp", "seq")),
            P(("dp", "seq"), None),
            P(("dp", "seq")),
            P(("dp", "seq")),
            P(("dp", "seq")),
            P(("dp", "seq"), None),
            P(("dp", "seq")),
            P(("dp", "seq"), None),
            P(("dp", "seq")),
            P(("dp", "seq")),
            P(("dp", "seq")),
        ),
        out_specs=(
            P("dp", "seq", None),
            P("dp", "seq", None),
            P(("dp", "seq"), None),
            P(("dp", "seq")),
            P(("dp", "seq")),
            P(("dp", "seq"), None),
            P(("dp", "seq")),
            P(("dp", "seq")),
            P(("dp", "seq")),
            P(("dp", "seq"), None),
            P(("dp", "seq")),
            P(("dp", "seq"), None),
            P(("dp", "seq")),
            P(("dp", "seq")),
            P(("dp", "seq")),
        ),
        check_vma=False,
    )
```
